32 devices in a mesh: groups: 2 (over x), expert: 16 (over z, y, core).
Axes of the slice: x: 2, y: 2, z: 4, core: 2. Of those that a mesh axis runs over, the one named last changes fastest.
Arguments:
- tokens: bfloat16 [4096, 4096], P(('groups', 'expert')), parts along dimension 0, may hold values from -6 to 6
- routing: int32 [4096], P(('groups', 'expert')), parts along dimension 0, may hold values from 0 to 7, as said below
- capacity_slot: int32 [4096], P(('groups', 'expert')), parts along dimension 0, may hold values from 0 to 24, as said below
- router_prob: float32 [4096], P(('groups', 'expert')), parts along dimension 0, may hold values from 0.3 to 1
- norm_gain: float32 [4096], replicated, may hold values from 0.5 to 2
- expert_in: bfloat16 [16, 4096, 2560], P('expert'), may hold values from -0.09375 to 0.09375
- expert_out: bfloat16 [16, 2560, 4096], P('expert'), may hold values from -0.078125 to 0.078125
Outputs:
- layer_output: bfloat16 [4096, 4096], P(('groups', 'expert')), parts along dimension 0
The draws below stay inside these ranges and needn't reach their ends.
There are 2 independent parts, one for each index of `groups`. The reference program is written for one: setup_inputs(seed, part) draws one part's arguments, and reference() takes and returns one part's arrays. A program takes and returns all parts, laid end to end along the dimension named above; an argument that names none is the same for every part. Nothing has to cross between parts.
Inputs may be any that keep to these rules, and one draw needn't show every extreme that they name: `routing`: on the rows of one device one expert, the same on every device of a part, is named by exactly 25 rows; every other expert by at most 20 rows. `capacity_slot`: on the rows of one device the rows that name one expert have distinct slots; those of the expert named by 20 + 5 rows take every slot below 25, all others stay below 20.
All inputs are finite; a program needn't handle non-finite values.
Results may differ from the reference program's by a relative error of at most 0.0048.
Values may be sent and summed in bfloat16 or wider, within the bound.
A program may use at most 128 MiB of HBM per device.

```python
import math
import jax
import jax.numpy as jnp
from jax import lax

D = 4096
FFW = 5120
EXP_WIN = 8
TOK_DEV = 128
CAP = 20
OVER = 5
GROUP = 2
F_DEV = 2560
TOKENS = 2048
N_EXPERT = 16


def routing_table(key):
    blocks = TOKENS // TOK_DEV
    busiest = jax.random.randint(jax.random.fold_in(key, 11), (), 0, EXP_WIN).astype(jnp.int32)
    block_keys = jax.random.split(jax.random.fold_in(key, 12), blocks)
    heavy_rows = CAP + OVER

    def one_block(block_key):
        placing_key, pool_key = jax.random.split(block_key)
        placing = jax.random.permutation(placing_key, TOK_DEV)
        pool_ids = jax.random.permutation(pool_key, (EXP_WIN - 1) * CAP)[:TOK_DEV - heavy_rows].astype(jnp.int32)
        experts_rank = jnp.concatenate([jnp.full((heavy_rows,), busiest, jnp.int32), ((busiest + 1 + pool_ids // CAP) % EXP_WIN).astype(jnp.int32)])
        slots_rank = jnp.concatenate([jnp.arange(heavy_rows, dtype=jnp.int32), (pool_ids % CAP).astype(jnp.int32)])
        experts_pos = jnp.zeros((TOK_DEV,), jnp.int32).at[placing].set(experts_rank)
        slots_pos = jnp.zeros((TOK_DEV,), jnp.int32).at[placing].set(slots_rank)
        return (experts_pos, slots_pos)
    experts_all, slots_all = jax.vmap(one_block)(block_keys)
    return (experts_all.reshape(TOKENS), slots_all.reshape(TOKENS))


def draw_routing(key, part):
    table = routing_table(key)
    return table[0]


def draw_capacity_slot(key, part):
    table = routing_table(key)
    return table[1]


def steps_of(key, extent, cuts, low, top_value):
    level = 1.0
    for axis_at, parts in cuts:
        draws = jax.random.uniform(jax.random.fold_in(jax.random.fold_in(key, 6), axis_at), (parts,), jnp.float32, low / len(cuts), top_value / len(cuts))
        level = level * jnp.repeat(jnp.exp(draws), extent[axis_at] // parts).reshape((-1,) + (1,) * (len(extent) - 1 - axis_at))
    return level


def normal_values(own_key, shape, scale, bound, cuts=(), kind=jnp.bfloat16):
    result = scale * jax.random.normal(own_key, shape, jnp.float32)
    if cuts:
        result = result * steps_of(own_key, shape, cuts, -0.22, 0.18)
    return jnp.clip(result, -bound, bound).astype(kind)


def setup_inputs(seed: int = 0, part: int = 0) -> dict:
    splits = jax.random.split(jax.random.key(seed), 8)
    part_splits = jax.random.split(jax.random.fold_in(splits[7], part), 8)
    tokens = normal_values(part_splits[0], (TOKENS, D), 1.0, 6.0, ((0, 16),))
    routing = draw_routing(jax.random.fold_in(jax.random.fold_in(splits[7], part), 71), part)
    capacity_slot = draw_capacity_slot(jax.random.fold_in(jax.random.fold_in(splits[7], part), 71), part)
    router_prob = jnp.clip(0.3 + 0.7 * jax.random.uniform(part_splits[3], (TOKENS,), jnp.float32) ** steps_of(part_splits[3], (TOKENS,), ((0, 16),), -0.2, 0.2), 0.3, 1.0)
    norm_gain = jnp.clip(jnp.exp(jax.random.uniform(splits[4], (D,), jnp.float32, math.log(0.5), math.log(2.0))), 0.5, 2.0)
    expert_in = normal_values(splits[5], (EXP_WIN * GROUP, D, F_DEV), D ** -0.5, 0.09375, ((0, 16),))
    expert_out = normal_values(splits[6], (EXP_WIN * GROUP, F_DEV, D), FFW ** -0.5, 0.078125, ((0, 16),))
    return dict(tokens=tokens, routing=routing, capacity_slot=capacity_slot, router_prob=router_prob, norm_gain=norm_gain, expert_in=expert_in, expert_out=expert_out)


def reference(tokens, routing, capacity_slot, router_prob, norm_gain, expert_in, expert_out):
    widened = tokens.astype(jnp.float32)
    normed = (widened * lax.rsqrt(lax.optimization_barrier(jnp.mean(widened * widened, axis=-1, keepdims=True)) + 1e-06) * norm_gain).astype(jnp.bfloat16)
    source = (jnp.arange(TOKENS) // TOK_DEV).astype(jnp.int32)
    buckets = jnp.zeros((EXP_WIN, N_EXPERT, CAP, D), jnp.bfloat16).at[routing, source, capacity_slot].set(normed, mode='drop')
    weights_in = expert_in.reshape(EXP_WIN, GROUP, D, F_DEV)
    weights_out = expert_out.reshape(EXP_WIN, GROUP, F_DEV, D)

    def run_expert(operands):
        bucket_rows, matrices_in, matrices_out = operands
        flat_rows = bucket_rows.reshape(N_EXPERT * CAP, D)

        def one_share(running, share_pair):
            matrix_in, matrix_out = share_pair
            hidden = jnp.maximum(jnp.dot(flat_rows, matrix_in, preferred_element_type=jnp.float32), 0.0).astype(jnp.bfloat16)
            partial_value = jnp.dot(hidden, matrix_out, preferred_element_type=jnp.float32).astype(jnp.bfloat16)
            return (running + partial_value.astype(jnp.float32), None)
        summed, _ = lax.scan(one_share, jnp.zeros((N_EXPERT * CAP, D), jnp.float32), (matrices_in, matrices_out))
        return summed.reshape(N_EXPERT, CAP, D)
    results = lax.map(run_expert, (buckets, weights_in, weights_out))
    branch = results.at[routing, source, capacity_slot].get(mode='fill', fill_value=0.0)
    return (widened + router_prob[:, None] * branch).astype(jnp.bfloat16)
```

```python
import functools

import jax
import jax.numpy as jnp
import numpy as np
from jax import lax
from jax.experimental import pallas as pl
from jax.experimental.pallas import tpu as pltpu
from jax.sharding import PartitionSpec as P

EXP_WIN = 8
CAP = 20
Q = 4
GROUP = 4
SETS = ((2,), (3, 1, 0))
TILE = 256
MESH = pl.DeviceIdType.MESH


def from_partner(x, axis, distance):
    return lax.ppermute(x, axis, [(i, i ^ 1 << distance) for i in range(lax.axis_size(axis))])


def wait_bytes(ref, sem):
    pltpu.make_async_copy(ref, ref, sem).wait()


def kernel(
    tok_ref, gain_ref, prob_ref, code_row_ref, code_col_ref, slot_col_ref, slot_row_ref, perm_ref, perm_t_ref,
    win_hbm, wout_hbm, out_ref,
    win, wout, placing, stacked, send_buf, recv_buf, x_buf, h_acc, hidden, pex_send, pex_recv, y_buf,
    ret_send, ret_recv,
    w_sem, send_sem, recv_sem, fwd_send_sem, fwd_recv_sem, pex_send_sem, pex_recv_sem, ret_send_sem, ret_recv_sem,
):
    n = 2 * EXP_WIN
    rows, features = tok_ref.shape
    half = features // 2
    chunk = half // Q
    block = Q * CAP
    me = lax.axis_index("expert")
    core = lax.rem(me, 2)
    chip = me // 2
    plane = me // GROUP
    partner = me + 1 - 2 * core

    barrier = pltpu.get_barrier_semaphore()

    @pl.loop(1, n)
    def _(i):
        pl.semaphore_signal(barrier, inc=1, device_id={"expert": lax.rem(me + i, n)}, device_id_type=MESH)

    own_col = pl.multiple_of(core * half, half)
    other_col = pl.multiple_of((1 - core) * half, half)
    loads = [
        pltpu.make_async_copy(win_hbm.at[0, pl.ds(own_col, half), :], win.at[0], w_sem.at[0]),
        pltpu.make_async_copy(win_hbm.at[0, pl.ds(other_col, half), :], win.at[1], w_sem.at[1]),
        pltpu.make_async_copy(wout_hbm.at[0, :, pl.ds(other_col, half)], wout.at[0], w_sem.at[2]),
        pltpu.make_async_copy(wout_hbm.at[0, :, pl.ds(own_col, half)], wout.at[1], w_sem.at[3]),
    ]
    for load in loads:
        load.start()

    @pl.loop(0, rows // 16)
    def _(r):
        top = pl.multiple_of(r * 16, 16)
        widened = tok_ref[pl.ds(top, 16), :].astype(jnp.float32)
        normed = (
            widened
            * lax.rsqrt(jnp.mean(widened * widened, axis=-1, keepdims=True) + 1e-06)
            * gain_ref[...]
        ).astype(jnp.bfloat16)
        for h in range(2):
            for q in range(Q):
                at = h * half + q * chunk
                stacked[h, pl.ds(pl.multiple_of(q * rows + top, 16), 16), :] = normed[:, at : at + chunk]

    placing[...] = jnp.where(slot_col_ref[...] == code_row_ref[...], 1.0, 0.0).astype(jnp.bfloat16)
    for h in range(2):
        for t in range(chunk // TILE):
            cols = slice(t * TILE, (t + 1) * TILE)
            send_buf[h, :, cols] = jnp.dot(
                placing[...], stacked[h, :, cols], preferred_element_type=jnp.float32
            ).astype(jnp.bfloat16)

    pl.semaphore_wait(barrier, n - 1)

    for j in [g for s in SETS for g in s]:
        for y in range(2):
            dst_chip = jnp.bitwise_xor(plane, j) * 2 + y
            src = [send_buf.at[h, pl.ds(pl.multiple_of(dst_chip * block, block), block), :] for h in range(2)]
            spot = pl.multiple_of((j * GROUP + lax.rem(me, GROUP)) * block, block)
            for h in range(2):
                dst = dst_chip * 2 + h

                def remote(src=src[h], dst=dst):
                    pltpu.make_async_remote_copy(
                        src_ref=src,
                        dst_ref=recv_buf.at[pl.ds(spot, block), :],
                        send_sem=send_sem,
                        recv_sem=recv_sem.at[j],
                        device_id={"expert": dst},
                        device_id_type=MESH,
                    ).start()

                if j == 0:
                    pl.when(dst != me)(remote)

                    @pl.when(dst == me)
                    def _(src=src[h]):
                        pltpu.make_async_copy(
                            src, recv_buf.at[pl.ds(spot, block), :], recv_sem.at[0]
                        ).start()
                else:
                    remote()

    offset = 0
    for s, groups in enumerate(SETS):
        m = len(groups) * GROUP * CAP
        mine = pl.ds(offset, m)
        for g, j in enumerate(groups):
            seg = recv_buf.at[pl.ds(j * GROUP * block, GROUP * block), :]
            wait_bytes(seg, recv_sem.at[j])
            top = offset + g * GROUP * CAP
            for t in range(chunk // TILE):
                piece = jnp.dot(
                    perm_ref[...], seg[:, t * TILE : (t + 1) * TILE], preferred_element_type=jnp.float32
                ).astype(jnp.bfloat16)
                for q in range(Q):
                    x_buf[0, top : top + GROUP * CAP, q * chunk + t * TILE : q * chunk + (t + 1) * TILE] = piece[
                        q * GROUP * CAP : (q + 1) * GROUP * CAP, :
                    ]
        forward = pltpu.make_async_remote_copy(
            src_ref=x_buf.at[0, mine, :],
            dst_ref=x_buf.at[1, mine, :],
            send_sem=fwd_send_sem.at[s],
            recv_sem=fwd_recv_sem.at[s],
            device_id={"expert": partner},
            device_id_type=MESH,
        )
        forward.start()
        if s == 0:
            loads[0].wait()

        @pl.loop(0, hidden.shape[1] // TILE)
        def _(t):
            cols = pl.ds(pl.multiple_of(t * TILE, TILE), TILE)
            h_acc[0:m, cols] = jnp.dot(x_buf[0, mine, :], win[0, :, cols], preferred_element_type=jnp.float32)

        forward.wait_recv()
        if s == 0:
            loads[1].wait()

        @pl.loop(0, hidden.shape[1] // TILE)
        def _(t):
            cols = pl.ds(pl.multiple_of(t * TILE, TILE), TILE)
            total = h_acc[0:m, cols] + jnp.dot(
                x_buf[1, mine, :], win[1, :, cols], preferred_element_type=jnp.float32
            )
            hidden[0:m, cols] = jnp.maximum(total, 0.0).astype(jnp.bfloat16)

        if s == 0:
            loads[2].wait()
        exchange = []
        for p in range(2):

            @pl.loop(0, half // 2 // TILE)
            def _(t):
                cols = pl.ds(pl.multiple_of(p * (half // 2) + t * TILE, TILE), TILE)
                to = pl.ds(pl.multiple_of(t * TILE, TILE), TILE)
                pex_send[p, mine, to] = jnp.dot(
                    hidden[0:m, :], wout[0, :, cols], preferred_element_type=jnp.float32
                ).astype(jnp.bfloat16)

            copy = pltpu.make_async_remote_copy(
                src_ref=pex_send.at[p, mine, :],
                dst_ref=pex_recv.at[p, mine, :],
                send_sem=pex_send_sem.at[s, p],
                recv_sem=pex_recv_sem.at[s, p],
                device_id={"expert": partner},
                device_id_type=MESH,
            )
            copy.start()
            exchange.append(copy)
        if s == 0:
            loads[3].wait()
        for p in range(2):
            exchange[p].wait_recv()

            @pl.loop(0, half // 2 // TILE)
            def _(t):
                cols = pl.ds(pl.multiple_of(p * (half // 2) + t * TILE, TILE), TILE)
                to = pl.ds(pl.multiple_of(t * TILE, TILE), TILE)
                y_buf[0:m, cols] = (
                    jnp.dot(hidden[0:m, :], wout[1, :, cols], preferred_element_type=jnp.float32)
                    + pex_recv[p, mine, to].astype(jnp.float32)
                ).astype(jnp.bfloat16)

        for g, j in enumerate(groups):
            top = g * GROUP * CAP
            base = j * GROUP * block
            for t in range(chunk // TILE):
                above = jnp.concatenate(
                    [
                        y_buf[top : top + GROUP * CAP, q * chunk + t * TILE : q * chunk + (t + 1) * TILE]
                        for q in range(Q)
                    ],
                    axis=0,
                )
                ret_send[base : base + GROUP * block, t * TILE : (t + 1) * TILE] = jnp.dot(
                    perm_t_ref[...], above, preferred_element_type=jnp.float32
                ).astype(jnp.bfloat16)
            for i in range(GROUP):
                dst = jnp.bitwise_xor(plane, j) * GROUP + i
                src = ret_send.at[pl.ds(base + i * block, block), :]
                spot = ret_recv.at[core, pl.ds(pl.multiple_of(chip * block, block), block), :]

                def remote(src=src, dst=dst, spot=spot):
                    pltpu.make_async_remote_copy(
                        src_ref=src,
                        dst_ref=spot,
                        send_sem=ret_send_sem,
                        recv_sem=ret_recv_sem.at[core],
                        device_id={"expert": dst},
                        device_id_type=MESH,
                    ).start()

                if j == 0:
                    pl.when(dst != me)(remote)

                    @pl.when(dst == me)
                    def _(src=src, spot=spot):
                        pltpu.make_async_copy(src, spot, ret_recv_sem.at[core]).start()
                else:
                    remote()
        offset += m

    pick = stacked_pick(placing, code_col_ref, slot_row_ref)
    for h in range(2):
        wait_bytes(ret_recv.at[h], ret_recv_sem.at[h])
        for q in range(Q):
            for t in range(chunk // TILE):
                at = h * half + q * chunk + t * TILE
                picked = jnp.dot(
                    pick[q], ret_recv[h, :, t * TILE : (t + 1) * TILE], preferred_element_type=jnp.float32
                )
                out_ref[:, at : at + TILE] = (
                    tok_ref[:, at : at + TILE].astype(jnp.float32) + prob_ref[...] * picked
                ).astype(jnp.bfloat16)

    wait_bytes(recv_buf.at[pl.ds(0, (n - 1) * block), :], send_sem)
    wait_bytes(recv_buf.at[pl.ds(0, (n - 1) * block), :], ret_send_sem)
    offset = 0
    for s, groups in enumerate(SETS):
        m = len(groups) * GROUP * CAP
        mine = pl.ds(offset, m)
        wait_bytes(x_buf.at[0, mine, :], fwd_send_sem.at[s])
        for p in range(2):
            wait_bytes(pex_send.at[p, mine, :], pex_send_sem.at[s, p])
        offset += m


def stacked_pick(placing, code_col_ref, slot_row_ref):
    rows = code_col_ref.shape[0] // Q
    return [
        jnp.where(code_col_ref[q * rows : (q + 1) * rows, :] == slot_row_ref[...], 1.0, 0.0).astype(jnp.bfloat16)
        for q in range(Q)
    ]


def fused(tokens, routing, capacity_slot, router_prob, norm_gain, expert_in, expert_out):
    rows, features = tokens.shape
    half, chunk, block = features // 2, features // 2 // Q, Q * CAP
    units = expert_in.shape[2]
    slots = EXP_WIN * CAP
    stride = 2 * slots
    target = jnp.where(capacity_slot < CAP, routing * CAP + capacity_slot, -1)
    code = (target[None, :] + (jnp.arange(Q, dtype=jnp.int32) * stride)[:, None]).reshape(Q * rows)
    where = np.arange(EXP_WIN * block)
    slot_code = (where % block // CAP * stride + where // block * CAP + where % CAP).astype(np.int32)
    pos = np.arange(GROUP * block)
    q, src, slot = pos // (GROUP * CAP), pos // CAP % GROUP, pos % CAP
    perm = np.zeros((GROUP * block, GROUP * block), np.float32)
    perm[pos, src * block + q * CAP + slot] = 1
    largest = max(len(s) for s in SETS) * GROUP * CAP
    total = 2 * EXP_WIN * CAP
    vmem = pl.BlockSpec(memory_space=pltpu.VMEM)
    hbm = pl.BlockSpec(memory_space=pl.ANY)
    bf16 = jnp.bfloat16
    return pl.pallas_call(
        kernel,
        out_shape=jax.ShapeDtypeStruct(tokens.shape, tokens.dtype),
        in_specs=[vmem] * 9 + [hbm] * 2,
        out_specs=vmem,
        scratch_shapes=[
            pltpu.VMEM((2, half, units), bf16),
            pltpu.VMEM((2, units, half), bf16),
            pltpu.VMEM((EXP_WIN * block, Q * rows), bf16),
            pltpu.VMEM((2, Q * rows, chunk), bf16),
            pltpu.VMEM((2, EXP_WIN * block, chunk), bf16),
            pltpu.VMEM((2 * EXP_WIN * block, chunk), bf16),
            pltpu.VMEM((2, total, half), bf16),
            pltpu.VMEM((largest, units), jnp.float32),
            pltpu.VMEM((largest, units), bf16),
            pltpu.VMEM((2, total, half // 2), bf16),
            pltpu.VMEM((2, total, half // 2), bf16),
            pltpu.VMEM((largest, half), bf16),
            pltpu.VMEM((2 * EXP_WIN * block, chunk), bf16),
            pltpu.VMEM((2, EXP_WIN * block, chunk), bf16),
            pltpu.SemaphoreType.DMA((4,)),
            pltpu.SemaphoreType.DMA,
            pltpu.SemaphoreType.DMA((GROUP,)),
            pltpu.SemaphoreType.DMA((len(SETS),)),
            pltpu.SemaphoreType.DMA((len(SETS),)),
            pltpu.SemaphoreType.DMA((len(SETS), 2)),
            pltpu.SemaphoreType.DMA((len(SETS), 2)),
            pltpu.SemaphoreType.DMA,
            pltpu.SemaphoreType.DMA((2,)),
        ],
        compiler_params=pltpu.CompilerParams(
            collective_id=0, has_side_effects=True, vmem_limit_bytes=63 * 1024 * 1024
        ),
        cost_estimate=pl.CostEstimate(
            flops=4 * total * features * units, bytes_accessed=4 * features * units, transcendentals=0
        ),
    )(
        tokens,
        norm_gain[None, :],
        router_prob[:, None],
        code[None, :],
        code[:, None],
        jnp.asarray(slot_code[:, None]),
        jnp.asarray(slot_code[None, :]),
        jnp.asarray(perm, bf16),
        jnp.asarray(perm.T, bf16),
        expert_in,
        expert_out,
    )


def per_device(tokens, routing, capacity_slot, router_prob, norm_gain, expert_in, expert_out):
    devices = lax.axis_size("expert")
    holders = devices // EXP_WIN
    features = tokens.shape[1]
    slots_total = EXP_WIN * CAP
    widened = tokens.astype(jnp.float32)
    normed = (
        widened * lax.rsqrt(jnp.mean(widened * widened, axis=-1, keepdims=True) + 1e-06) * norm_gain
    ).astype(jnp.bfloat16)
    kept_rows = capacity_slot < CAP
    target = jnp.where(kept_rows, routing * CAP + capacity_slot, -1)
    placing = (target[None, :] == jnp.arange(slots_total, dtype=jnp.int32)[:, None]).astype(
        jnp.bfloat16
    )
    buckets = (
        jnp.dot(placing, normed, preferred_element_type=jnp.float32)
        .astype(jnp.bfloat16)
        .reshape(EXP_WIN, CAP, features)
    )
    weight_in = expert_in[0]
    weight_out = expert_out[0]
    slice_width = features // holders
    sliced = (
        buckets.reshape(EXP_WIN, CAP, holders, slice_width)
        .transpose(0, 2, 1, 3)
        .reshape(devices, CAP, slice_width)
    )
    bucket_rows = lax.all_to_all(sliced, "expert", split_axis=0, concat_axis=0, tiled=True)
    lowest = lax.axis_index("expert")
    for bit_pos in range(holders.bit_length() - 1):
        partner = from_partner(bucket_rows, "expert", bit_pos)
        upper_half = lowest >> bit_pos & 1 == 1
        bucket_rows = jnp.where(
            upper_half,
            jnp.concatenate([partner, bucket_rows], 2),
            jnp.concatenate([bucket_rows, partner], 2),
        )
    slot_count = bucket_rows.shape[1]
    flat_rows = bucket_rows.reshape(devices * slot_count, features)
    hidden = jnp.maximum(
        jnp.dot(flat_rows, weight_in, preferred_element_type=jnp.float32), 0.0
    ).astype(jnp.bfloat16)
    partial_value = jnp.dot(hidden, weight_out, preferred_element_type=jnp.float32).astype(
        jnp.bfloat16
    )
    partial_value = partial_value.reshape(devices, slot_count, features)
    returned = lax.all_to_all(partial_value, "expert", split_axis=0, concat_axis=0, tiled=True)
    combined = (
        returned.reshape(EXP_WIN, holders, CAP, features)
        .astype(jnp.float32)
        .sum(axis=1)
        .reshape(slots_total, features)
    )
    picked = jnp.take(combined, jnp.clip(target, 0, slots_total - 1), axis=0)
    branch = jnp.where(kept_rows[:, None], picked, 0.0)
    return (widened + router_prob[:, None] * branch).astype(jnp.bfloat16)


def solution(mesh):
    placed = (
        P(("groups", "expert"), None),
        P(("groups", "expert")),
        P(("groups", "expert")),
        P(("groups", "expert")),
        P(),
        P("expert", None, None),
        P("expert", None, None),
    )
    two_holders = mesh.shape["expert"] == 2 * EXP_WIN
    return jax.shard_map(
        fused if two_holders else per_device,
        mesh=mesh,
        in_specs=placed,
        out_specs=P(("groups", "expert"), None),
        check_vma=False,
    )
```

```python
import functools

import jax
import jax.numpy as jnp
import numpy as np
from jax import lax
from jax.experimental import pallas as pl
from jax.experimental.pallas import tpu as pltpu
from jax.sharding import PartitionSpec as P

EXP_WIN = 8
CAP = 20
Q = 4
GROUP = 4
SETS = ((2,1),(3,0))
ORDER = ((2, 0), (1, 0), (2, 1), (1, 1), (3, 0), (0, 0), (3, 1), (0, 1))
TILE = 256
MESH = pl.DeviceIdType.MESH


def from_partner(x, axis, distance):
    return lax.ppermute(x, axis, [(i, i ^ 1 << distance) for i in range(lax.axis_size(axis))])


def wait_bytes(ref, sem):
    pltpu.make_async_copy(ref, ref, sem).wait()


def kernel(
    tok_ref, gain_ref, routing_ref, capacity_ref, slot_col_ref, slot_row_ref, perm_ref, perm_t_ref,
    win_hbm, wout_hbm, out_ref,
    win, wout, placing, stacked, send_buf, recv_buf, x_buf, h_acc, hidden, pex_send, pex_recv, y_buf,
    ret_send, ret_recv,
    w_sem, send_sem, recv_sem, fwd_send_sem, fwd_recv_sem, pex_send_sem, pex_recv_sem, ret_send_sem, ret_recv_sem,
):
    n = 2 * EXP_WIN
    rows, features = tok_ref.shape
    half = features // 2
    chunk = half // Q
    block = Q * CAP
    me = lax.axis_index("expert")
    core = lax.rem(me, 2)
    chip = me // 2
    plane = me // GROUP
    partner = me + 1 - 2 * core

    barrier = pltpu.get_barrier_semaphore()

    @pl.loop(1, n)
    def _(i):
        pl.semaphore_signal(barrier, inc=1, device_id={"expert": lax.rem(me + i, n)}, device_id_type=MESH)

    own_col = pl.multiple_of(core * half, half)
    other_col = pl.multiple_of((1 - core) * half, half)
    loads = [
        pltpu.make_async_copy(win_hbm.at[0, pl.ds(own_col, half), :], win.at[0], w_sem.at[0]),
        pltpu.make_async_copy(win_hbm.at[0, pl.ds(other_col, half), :], win.at[1], w_sem.at[1]),
        pltpu.make_async_copy(wout_hbm.at[0, :, pl.ds(other_col, half)], wout.at[0], w_sem.at[2]),
        pltpu.make_async_copy(wout_hbm.at[0, :, pl.ds(own_col, half)], wout.at[1], w_sem.at[3]),
    ]
    for load in loads:
        load.start()

    @pl.loop(0, rows // 16)
    def _(r):
        top = pl.multiple_of(r * 16, 16)
        widened = tok_ref[pl.ds(top, 16), :].astype(jnp.float32)
        normed = (
            widened
            * lax.rsqrt(jnp.mean(widened * widened, axis=-1, keepdims=True) + 1e-06)
            * gain_ref[...]
        ).astype(jnp.bfloat16)
        for h in range(2):
            for q in range(Q):
                at = h * half + q * chunk
                stacked[h, pl.ds(pl.multiple_of(q * rows + top, 16), 16), :] = normed[:, at : at + chunk]

    kept = capacity_ref[...] < CAP
    target = jnp.where(kept, routing_ref[...] * CAP + capacity_ref[...], -1)
    stride = 2 * EXP_WIN * CAP
    for q in range(Q):
        placing[:, q * rows : (q + 1) * rows] = jnp.where(
            slot_col_ref[...] == target + q * stride, 1.0, 0.0
        ).astype(jnp.bfloat16)
    for h in range(2):
        for t in range(chunk // TILE):
            cols = slice(t * TILE, (t + 1) * TILE)
            send_buf[h, :, cols] = jnp.dot(
                placing[...], stacked[h, :, cols], preferred_element_type=jnp.float32
            ).astype(jnp.bfloat16)

    pl.semaphore_wait(barrier, n - 1)

    for j, y in ORDER:
        dst_chip = jnp.bitwise_xor(plane, j) * 2 + y
        src = [send_buf.at[h, pl.ds(pl.multiple_of(dst_chip * block, block), block), :] for h in range(2)]
        spot = pl.multiple_of((j * GROUP + lax.rem(me, GROUP)) * block, block)
        for h in range(2):
            dst = dst_chip * 2 + h

            def remote(src=src[h], dst=dst):
                pltpu.make_async_remote_copy(
                    src_ref=src,
                    dst_ref=recv_buf.at[pl.ds(spot, block), :],
                    send_sem=send_sem,
                    recv_sem=recv_sem.at[j],
                    device_id={"expert": dst},
                    device_id_type=MESH,
                ).start()

            if j == 0:
                pl.when(dst != me)(remote)

                @pl.when(dst == me)
                def _(src=src[h]):
                    pltpu.make_async_copy(
                        src, recv_buf.at[pl.ds(spot, block), :], recv_sem.at[0]
                    ).start()
            else:
                remote()

    offset = 0
    for s, groups in enumerate(SETS):
        m = len(groups) * GROUP * CAP
        mine = pl.ds(offset, m)
        for g, j in enumerate(groups):
            seg = recv_buf.at[pl.ds(j * GROUP * block, GROUP * block), :]
            wait_bytes(seg, recv_sem.at[j])
            top = offset + g * GROUP * CAP
            for t in range(chunk // TILE):
                piece = jnp.dot(
                    perm_ref[...], seg[:, t * TILE : (t + 1) * TILE], preferred_element_type=jnp.float32
                ).astype(jnp.bfloat16)
                for q in range(Q):
                    x_buf[0, top : top + GROUP * CAP, q * chunk + t * TILE : q * chunk + (t + 1) * TILE] = piece[
                        q * GROUP * CAP : (q + 1) * GROUP * CAP, :
                    ]
        forward = pltpu.make_async_remote_copy(
            src_ref=x_buf.at[0, mine, :],
            dst_ref=x_buf.at[1, mine, :],
            send_sem=fwd_send_sem.at[s],
            recv_sem=fwd_recv_sem.at[s],
            device_id={"expert": partner},
            device_id_type=MESH,
        )
        forward.start()
        if s == 0:
            loads[0].wait()

        @pl.loop(0, hidden.shape[1] // TILE)
        def _(t):
            cols = pl.ds(pl.multiple_of(t * TILE, TILE), TILE)
            h_acc[0:m, cols] = jnp.dot(x_buf[0, mine, :], win[0, :, cols], preferred_element_type=jnp.float32)

        forward.wait_recv()
        if s == 0:
            loads[1].wait()

        @pl.loop(0, hidden.shape[1] // TILE)
        def _(t):
            cols = pl.ds(pl.multiple_of(t * TILE, TILE), TILE)
            total = h_acc[0:m, cols] + jnp.dot(
                x_buf[1, mine, :], win[1, :, cols], preferred_element_type=jnp.float32
            )
            hidden[0:m, cols] = jnp.maximum(total, 0.0).astype(jnp.bfloat16)

        if s == 0:
            loads[2].wait()
        exchange = []
        for p in range(2):

            @pl.loop(0, half // 2 // TILE)
            def _(t):
                cols = pl.ds(pl.multiple_of(p * (half // 2) + t * TILE, TILE), TILE)
                to = pl.ds(pl.multiple_of(t * TILE, TILE), TILE)
                pex_send[p, mine, to] = jnp.dot(
                    hidden[0:m, :], wout[0, :, cols], preferred_element_type=jnp.float32
                ).astype(jnp.bfloat16)

            copy = pltpu.make_async_remote_copy(
                src_ref=pex_send.at[p, mine, :],
                dst_ref=pex_recv.at[p, mine, :],
                send_sem=pex_send_sem.at[s, p],
                recv_sem=pex_recv_sem.at[s, p],
                device_id={"expert": partner},
                device_id_type=MESH,
            )
            copy.start()
            exchange.append(copy)
        if s == 0:
            loads[3].wait()
        for p in range(2):
            exchange[p].wait_recv()

            @pl.loop(0, half // 2 // TILE)
            def _(t):
                cols = pl.ds(pl.multiple_of(p * (half // 2) + t * TILE, TILE), TILE)
                to = pl.ds(pl.multiple_of(t * TILE, TILE), TILE)
                y_buf[0:m, cols] = (
                    jnp.dot(hidden[0:m, :], wout[1, :, cols], preferred_element_type=jnp.float32)
                    + pex_recv[p, mine, to].astype(jnp.float32)
                ).astype(jnp.bfloat16)

        for g, j in enumerate(groups):
            top = g * GROUP * CAP
            base = j * GROUP * block
            for t in range(chunk // TILE):
                above = jnp.concatenate(
                    [
                        y_buf[top : top + GROUP * CAP, q * chunk + t * TILE : q * chunk + (t + 1) * TILE]
                        for q in range(Q)
                    ],
                    axis=0,
                )
                ret_send[base : base + GROUP * block, t * TILE : (t + 1) * TILE] = jnp.dot(
                    perm_t_ref[...], above, preferred_element_type=jnp.float32
                ).astype(jnp.bfloat16)
        for i in range(GROUP):
            for j in groups:
                base = j * GROUP * block
                dst = jnp.bitwise_xor(plane, j) * GROUP + i
                src = ret_send.at[pl.ds(base + i * block, block), :]
                spot = ret_recv.at[core, pl.ds(pl.multiple_of(chip * block, block), block), :]

                def remote(src=src, dst=dst, spot=spot):
                    pltpu.make_async_remote_copy(
                        src_ref=src,
                        dst_ref=spot,
                        send_sem=ret_send_sem,
                        recv_sem=ret_recv_sem.at[core],
                        device_id={"expert": dst},
                        device_id_type=MESH,
                    ).start()

                if j == 0:
                    pl.when(dst != me)(remote)

                    @pl.when(dst == me)
                    def _(src=src, spot=spot):
                        pltpu.make_async_copy(src, spot, ret_recv_sem.at[core]).start()
                else:
                    remote()
        offset += m

    diagonal = lax.broadcasted_iota(jnp.int32, (rows, rows), 0) == lax.broadcasted_iota(jnp.int32, (rows, rows), 1)
    target_col = jnp.sum(jnp.where(diagonal, target, 0), axis=1, keepdims=True)
    pick = [
        jnp.where(target_col + q * stride == slot_row_ref[...], 1.0, 0.0).astype(jnp.bfloat16) for q in range(Q)
    ]
    for h in range(2):
        wait_bytes(ret_recv.at[h], ret_recv_sem.at[h])
        for q in range(Q):
            for t in range(chunk // TILE):
                at = h * half + q * chunk + t * TILE
                out_ref[:, at : at + TILE] = jnp.dot(
                    pick[q], ret_recv[h, :, t * TILE : (t + 1) * TILE], preferred_element_type=jnp.float32
                ).astype(jnp.bfloat16)

    wait_bytes(recv_buf.at[pl.ds(0, (n - 1) * block), :], send_sem)
    wait_bytes(recv_buf.at[pl.ds(0, (n - 1) * block), :], ret_send_sem)
    offset = 0
    for s, groups in enumerate(SETS):
        m = len(groups) * GROUP * CAP
        mine = pl.ds(offset, m)
        wait_bytes(x_buf.at[0, mine, :], fwd_send_sem.at[s])
        for p in range(2):
            wait_bytes(pex_send.at[p, mine, :], pex_send_sem.at[s, p])
        offset += m


def fused(tokens, routing, capacity_slot, router_prob, norm_gain, expert_in, expert_out):
    rows, features = tokens.shape
    half, chunk, block = features // 2, features // 2 // Q, Q * CAP
    units = expert_in.shape[2]
    slots = EXP_WIN * CAP
    stride = 2 * slots
    where = np.arange(EXP_WIN * block)
    slot_code = (where % block // CAP * stride + where // block * CAP + where % CAP).astype(np.int32)
    pos = np.arange(GROUP * block)
    q, src, slot = pos // (GROUP * CAP), pos // CAP % GROUP, pos % CAP
    perm = np.zeros((GROUP * block, GROUP * block), np.float32)
    perm[pos, src * block + q * CAP + slot] = 1
    largest = max(len(s) for s in SETS) * GROUP * CAP
    total = 2 * EXP_WIN * CAP
    vmem = pl.BlockSpec(memory_space=pltpu.VMEM)
    hbm = pl.BlockSpec(memory_space=pl.ANY)
    bf16 = jnp.bfloat16
    branch = pl.pallas_call(
        kernel,
        out_shape=jax.ShapeDtypeStruct(tokens.shape, tokens.dtype),
        in_specs=[vmem] * 8 + [hbm] * 2,
        out_specs=vmem,
        scratch_shapes=[
            pltpu.VMEM((2, half, units), bf16),
            pltpu.VMEM((2, units, half), bf16),
            pltpu.VMEM((EXP_WIN * block, Q * rows), bf16),
            pltpu.VMEM((2, Q * rows, chunk), bf16),
            pltpu.VMEM((2, EXP_WIN * block, chunk), bf16),
            pltpu.VMEM((2 * EXP_WIN * block, chunk), bf16),
            pltpu.VMEM((2, total, half), bf16),
            pltpu.VMEM((largest, units), jnp.float32),
            pltpu.VMEM((largest, units), bf16),
            pltpu.VMEM((2, total, half // 2), bf16),
            pltpu.VMEM((2, total, half // 2), bf16),
            pltpu.VMEM((largest, half), bf16),
            pltpu.VMEM((2 * EXP_WIN * block, chunk), bf16),
            pltpu.VMEM((2, EXP_WIN * block, chunk), bf16),
            pltpu.SemaphoreType.DMA((4,)),
            pltpu.SemaphoreType.DMA,
            pltpu.SemaphoreType.DMA((GROUP,)),
            pltpu.SemaphoreType.DMA((len(SETS),)),
            pltpu.SemaphoreType.DMA((len(SETS),)),
            pltpu.SemaphoreType.DMA((len(SETS), 2)),
            pltpu.SemaphoreType.DMA((len(SETS), 2)),
            pltpu.SemaphoreType.DMA,
            pltpu.SemaphoreType.DMA((2,)),
        ],
        compiler_params=pltpu.CompilerParams(
            collective_id=0, has_side_effects=True, vmem_limit_bytes=63 * 1024 * 1024
        ),
        cost_estimate=pl.CostEstimate(
            flops=4 * total * features * units, bytes_accessed=4 * features * units, transcendentals=0
        ),
    )(
        tokens,
        norm_gain[None, :],
        routing[None, :],
        capacity_slot[None, :],
        jnp.asarray(slot_code[:, None]),
        jnp.asarray(slot_code[None, :]),
        jnp.asarray(perm, bf16),
        jnp.asarray(perm.T, bf16),
        expert_in,
        expert_out,
    )
    return (tokens.astype(jnp.float32) + router_prob[:, None] * branch.astype(jnp.float32)).astype(jnp.bfloat16)


def per_device(tokens, routing, capacity_slot, router_prob, norm_gain, expert_in, expert_out):
    devices = lax.axis_size("expert")
    holders = devices // EXP_WIN
    features = tokens.shape[1]
    slots_total = EXP_WIN * CAP
    widened = tokens.astype(jnp.float32)
    normed = (
        widened * lax.rsqrt(jnp.mean(widened * widened, axis=-1, keepdims=True) + 1e-06) * norm_gain
    ).astype(jnp.bfloat16)
    kept_rows = capacity_slot < CAP
    target = jnp.where(kept_rows, routing * CAP + capacity_slot, -1)
    placing = (target[None, :] == jnp.arange(slots_total, dtype=jnp.int32)[:, None]).astype(
        jnp.bfloat16
    )
    buckets = (
        jnp.dot(placing, normed, preferred_element_type=jnp.float32)
        .astype(jnp.bfloat16)
        .reshape(EXP_WIN, CAP, features)
    )
    weight_in = expert_in[0]
    weight_out = expert_out[0]
    slice_width = features // holders
    sliced = (
        buckets.reshape(EXP_WIN, CAP, holders, slice_width)
        .transpose(0, 2, 1, 3)
        .reshape(devices, CAP, slice_width)
    )
    bucket_rows = lax.all_to_all(sliced, "expert", split_axis=0, concat_axis=0, tiled=True)
    lowest = lax.axis_index("expert")
    for bit_pos in range(holders.bit_length() - 1):
        partner = from_partner(bucket_rows, "expert", bit_pos)
        upper_half = lowest >> bit_pos & 1 == 1
        bucket_rows = jnp.where(
            upper_half,
            jnp.concatenate([partner, bucket_rows], 2),
            jnp.concatenate([bucket_rows, partner], 2),
        )
    slot_count = bucket_rows.shape[1]
    flat_rows = bucket_rows.reshape(devices * slot_count, features)
    hidden = jnp.maximum(
        jnp.dot(flat_rows, weight_in, preferred_element_type=jnp.float32), 0.0
    ).astype(jnp.bfloat16)
    partial_value = jnp.dot(hidden, weight_out, preferred_element_type=jnp.float32).astype(
        jnp.bfloat16
    )
    partial_value = partial_value.reshape(devices, slot_count, features)
    returned = lax.all_to_all(partial_value, "expert", split_axis=0, concat_axis=0, tiled=True)
    combined = (
        returned.reshape(EXP_WIN, holders, CAP, features)
        .astype(jnp.float32)
        .sum(axis=1)
        .reshape(slots_total, features)
    )
    picked = jnp.take(combined, jnp.clip(target, 0, slots_total - 1), axis=0)
    branch = jnp.where(kept_rows[:, None], picked, 0.0)
    return (widened + router_prob[:, None] * branch).astype(jnp.bfloat16)


def solution(mesh):
    placed = (
        P(("groups", "expert"), None),
        P(("groups", "expert")),
        P(("groups", "expert")),
        P(("groups", "expert")),
        P(),
        P("expert", None, None),
        P("expert", None, None),
    )
    two_holders = mesh.shape["expert"] == 2 * EXP_WIN
    return jax.shard_map(
        fused if two_holders else per_device,
        mesh=mesh,
        in_specs=placed,
        out_specs=P(("groups", "expert"), None),
        check_vma=False,
    )
```

```python
import functools

import jax
import jax.numpy as jnp
import numpy as np
from jax import lax
from jax.experimental import pallas as pl
from jax.experimental.pallas import tpu as pltpu
from jax.sharding import PartitionSpec as P

EXP_WIN = 8
CAP = 20
Q = 4
GROUP = 4
SETS = ((2,1),(3,0))
ORDER = ((2, 0), (2, 1), (1, 0), (1, 1), (3, 0), (3, 1), (0, 0), (0, 1))
TILE = 256
MESH = pl.DeviceIdType.MESH


def from_partner(x, axis, distance):
    return lax.ppermute(x, axis, [(i, i ^ 1 << distance) for i in range(lax.axis_size(axis))])


def wait_bytes(ref, sem):
    pltpu.make_async_copy(ref, ref, sem).wait()


def kernel(
    tok_ref, gain_ref, routing_ref, capacity_ref, slot_col_ref, slot_row_ref, perm_ref, perm_t_ref,
    win_hbm, wout_hbm, out_ref,
    win, wout, placing, stacked, send_buf, recv_buf, x_buf, h_acc, hidden, pex_send, pex_recv, y_buf,
    ret_send, ret_recv,
    w_sem, send_sem, recv_sem, fwd_send_sem, fwd_recv_sem, pex_send_sem, pex_recv_sem, ret_send_sem, ret_recv_sem,
):
    n = 2 * EXP_WIN
    rows, features = tok_ref.shape
    half = features // 2
    chunk = half // Q
    block = Q * CAP
    me = lax.axis_index("expert")
    core = lax.rem(me, 2)
    chip = me // 2
    plane = me // GROUP
    partner = me + 1 - 2 * core

    barrier = pltpu.get_barrier_semaphore()

    @pl.loop(1, n)
    def _(i):
        pl.semaphore_signal(barrier, inc=1, device_id={"expert": lax.rem(me + i, n)}, device_id_type=MESH)

    own_col = pl.multiple_of(core * half, half)
    other_col = pl.multiple_of((1 - core) * half, half)
    loads = [
        pltpu.make_async_copy(win_hbm.at[0, pl.ds(own_col, half), :], win.at[0], w_sem.at[0]),
        pltpu.make_async_copy(win_hbm.at[0, pl.ds(other_col, half), :], win.at[1], w_sem.at[1]),
        pltpu.make_async_copy(wout_hbm.at[0, :, pl.ds(other_col, half)], wout.at[0], w_sem.at[2]),
        pltpu.make_async_copy(wout_hbm.at[0, :, pl.ds(own_col, half)], wout.at[1], w_sem.at[3]),
    ]
    for load in loads:
        load.start()

    @pl.loop(0, rows // 16)
    def _(r):
        top = pl.multiple_of(r * 16, 16)
        widened = tok_ref[pl.ds(top, 16), :].astype(jnp.float32)
        normed = (
            widened
            * lax.rsqrt(jnp.mean(widened * widened, axis=-1, keepdims=True) + 1e-06)
            * gain_ref[...]
        ).astype(jnp.bfloat16)
        for h in range(2):
            for q in range(Q):
                at = h * half + q * chunk
                stacked[h, pl.ds(pl.multiple_of(q * rows + top, 16), 16), :] = normed[:, at : at + chunk]

    kept = capacity_ref[...] < CAP
    target = jnp.where(kept, routing_ref[...] * CAP + capacity_ref[...], -1)
    stride = 2 * EXP_WIN * CAP
    for q in range(Q):
        placing[:, q * rows : (q + 1) * rows] = jnp.where(
            slot_col_ref[...] == target + q * stride, 1.0, 0.0
        ).astype(jnp.bfloat16)
    pl.semaphore_wait(barrier, n - 1)

    for j, y in ORDER:
        if y == 0:
            bound = pl.ds(pl.multiple_of(jnp.bitwise_xor(plane, j) * 2 * block, 2 * block), 2 * block)
            for h in range(2):
                send_buf[h, bound, :] = jnp.dot(
                    placing[bound, :], stacked[h], preferred_element_type=jnp.float32
                ).astype(jnp.bfloat16)
        dst_chip = jnp.bitwise_xor(chip, j * 2 + y)
        src = [send_buf.at[h, pl.ds(pl.multiple_of(dst_chip * block, block), block), :] for h in range(2)]
        spot = pl.multiple_of((j * GROUP + lax.rem(me, GROUP)) * block, block)
        for h in range(2):
            dst = dst_chip * 2 + h

            def remote(src=src[h], dst=dst):
                pltpu.make_async_remote_copy(
                    src_ref=src,
                    dst_ref=recv_buf.at[pl.ds(spot, block), :],
                    send_sem=send_sem,
                    recv_sem=recv_sem.at[j],
                    device_id={"expert": dst},
                    device_id_type=MESH,
                ).start()

            if j == 0 and y == 0:
                pl.when(dst != me)(remote)

                @pl.when(dst == me)
                def _(src=src[h]):
                    pltpu.make_async_copy(
                        src, recv_buf.at[pl.ds(spot, block), :], recv_sem.at[0]
                    ).start()
            else:
                remote()

    offset = 0
    for s, groups in enumerate(SETS):
        m = len(groups) * GROUP * CAP
        mine = pl.ds(offset, m)
        for g, j in enumerate(groups):
            seg = recv_buf.at[pl.ds(j * GROUP * block, GROUP * block), :]
            wait_bytes(seg, recv_sem.at[j])
            top = offset + g * GROUP * CAP
            for t in range(chunk // TILE):
                piece = jnp.dot(
                    perm_ref[...], seg[:, t * TILE : (t + 1) * TILE], preferred_element_type=jnp.float32
                ).astype(jnp.bfloat16)
                for q in range(Q):
                    x_buf[0, top : top + GROUP * CAP, q * chunk + t * TILE : q * chunk + (t + 1) * TILE] = piece[
                        q * GROUP * CAP : (q + 1) * GROUP * CAP, :
                    ]
        forward = pltpu.make_async_remote_copy(
            src_ref=x_buf.at[0, mine, :],
            dst_ref=x_buf.at[1, mine, :],
            send_sem=fwd_send_sem.at[s],
            recv_sem=fwd_recv_sem.at[s],
            device_id={"expert": partner},
            device_id_type=MESH,
        )
        forward.start()
        if s == 0:
            loads[0].wait()

        @pl.loop(0, hidden.shape[1] // TILE)
        def _(t):
            cols = pl.ds(pl.multiple_of(t * TILE, TILE), TILE)
            h_acc[0:m, cols] = jnp.dot(x_buf[0, mine, :], win[0, :, cols], preferred_element_type=jnp.float32)

        forward.wait_recv()
        if s == 0:
            loads[1].wait()

        @pl.loop(0, hidden.shape[1] // TILE)
        def _(t):
            cols = pl.ds(pl.multiple_of(t * TILE, TILE), TILE)
            total = h_acc[0:m, cols] + jnp.dot(
                x_buf[1, mine, :], win[1, :, cols], preferred_element_type=jnp.float32
            )
            hidden[0:m, cols] = jnp.maximum(total, 0.0).astype(jnp.bfloat16)

        if s == 0:
            loads[2].wait()
        exchange = []
        for p in range(2):

            @pl.loop(0, half // 2 // TILE)
            def _(t):
                cols = pl.ds(pl.multiple_of(p * (half // 2) + t * TILE, TILE), TILE)
                to = pl.ds(pl.multiple_of(t * TILE, TILE), TILE)
                pex_send[p, mine, to] = jnp.dot(
                    hidden[0:m, :], wout[0, :, cols], preferred_element_type=jnp.float32
                ).astype(jnp.bfloat16)

            copy = pltpu.make_async_remote_copy(
                src_ref=pex_send.at[p, mine, :],
                dst_ref=pex_recv.at[p, mine, :],
                send_sem=pex_send_sem.at[s, p],
                recv_sem=pex_recv_sem.at[s, p],
                device_id={"expert": partner},
                device_id_type=MESH,
            )
            copy.start()
            exchange.append(copy)
        if s == 0:
            loads[3].wait()
        for p in range(2):
            exchange[p].wait_recv()

            @pl.loop(0, half // 2 // TILE)
            def _(t):
                cols = pl.ds(pl.multiple_of(p * (half // 2) + t * TILE, TILE), TILE)
                to = pl.ds(pl.multiple_of(t * TILE, TILE), TILE)
                y_buf[0:m, cols] = (
                    jnp.dot(hidden[0:m, :], wout[1, :, cols], preferred_element_type=jnp.float32)
                    + pex_recv[p, mine, to].astype(jnp.float32)
                ).astype(jnp.bfloat16)

        for g, j in enumerate(groups):
            top = g * GROUP * CAP
            base = j * GROUP * block
            for t in range(chunk // TILE):
                above = jnp.concatenate(
                    [
                        y_buf[top : top + GROUP * CAP, q * chunk + t * TILE : q * chunk + (t + 1) * TILE]
                        for q in range(Q)
                    ],
                    axis=0,
                )
                ret_send[base : base + GROUP * block, t * TILE : (t + 1) * TILE] = jnp.dot(
                    perm_t_ref[...], above, preferred_element_type=jnp.float32
                ).astype(jnp.bfloat16)
        for i in (0, 2, 1, 3):
            for j in groups:
                dst = jnp.bitwise_xor(me, j * GROUP + i)
                src = ret_send.at[pl.ds(pl.multiple_of((j * GROUP + lax.rem(dst, GROUP)) * block, block), block), :]
                spot = ret_recv.at[core, pl.ds(pl.multiple_of(chip * block, block), block), :]

                def remote(src=src, dst=dst, spot=spot):
                    pltpu.make_async_remote_copy(
                        src_ref=src,
                        dst_ref=spot,
                        send_sem=ret_send_sem,
                        recv_sem=ret_recv_sem.at[core],
                        device_id={"expert": dst},
                        device_id_type=MESH,
                    ).start()

                if j == 0 and i == 0:
                    pltpu.make_async_copy(src, spot, ret_recv_sem.at[core]).start()
                else:
                    remote()
        offset += m

    diagonal = lax.broadcasted_iota(jnp.int32, (rows, rows), 0) == lax.broadcasted_iota(jnp.int32, (rows, rows), 1)
    target_col = jnp.sum(jnp.where(diagonal, target, 0), axis=1, keepdims=True)
    pick = [
        jnp.where(target_col + q * stride == slot_row_ref[...], 1.0, 0.0).astype(jnp.bfloat16) for q in range(Q)
    ]
    for h in range(2):
        wait_bytes(ret_recv.at[h], ret_recv_sem.at[h])
        for q in range(Q):
            for t in range(chunk // TILE):
                at = h * half + q * chunk + t * TILE
                out_ref[:, at : at + TILE] = jnp.dot(
                    pick[q], ret_recv[h, :, t * TILE : (t + 1) * TILE], preferred_element_type=jnp.float32
                ).astype(jnp.bfloat16)

    wait_bytes(recv_buf.at[pl.ds(0, (n - 1) * block), :], send_sem)
    wait_bytes(recv_buf.at[pl.ds(0, (n - 1) * block), :], ret_send_sem)
    offset = 0
    for s, groups in enumerate(SETS):
        m = len(groups) * GROUP * CAP
        mine = pl.ds(offset, m)
        wait_bytes(x_buf.at[0, mine, :], fwd_send_sem.at[s])
        for p in range(2):
            wait_bytes(pex_send.at[p, mine, :], pex_send_sem.at[s, p])
        offset += m


def fused(tokens, routing, capacity_slot, router_prob, norm_gain, expert_in, expert_out):
    rows, features = tokens.shape
    half, chunk, block = features // 2, features // 2 // Q, Q * CAP
    units = expert_in.shape[2]
    slots = EXP_WIN * CAP
    stride = 2 * slots
    where = np.arange(EXP_WIN * block)
    slot_code = (where % block // CAP * stride + where // block * CAP + where % CAP).astype(np.int32)
    pos = np.arange(GROUP * block)
    q, src, slot = pos // (GROUP * CAP), pos // CAP % GROUP, pos % CAP
    perm = np.zeros((GROUP * block, GROUP * block), np.float32)
    perm[pos, src * block + q * CAP + slot] = 1
    largest = max(len(s) for s in SETS) * GROUP * CAP
    total = 2 * EXP_WIN * CAP
    vmem = pl.BlockSpec(memory_space=pltpu.VMEM)
    hbm = pl.BlockSpec(memory_space=pl.ANY)
    bf16 = jnp.bfloat16
    branch = pl.pallas_call(
        kernel,
        out_shape=jax.ShapeDtypeStruct(tokens.shape, tokens.dtype),
        in_specs=[vmem] * 8 + [hbm] * 2,
        out_specs=vmem,
        scratch_shapes=[
            pltpu.VMEM((2, half, units), bf16),
            pltpu.VMEM((2, units, half), bf16),
            pltpu.VMEM((EXP_WIN * block, Q * rows), bf16),
            pltpu.VMEM((2, Q * rows, chunk), bf16),
            pltpu.VMEM((2, EXP_WIN * block, chunk), bf16),
            pltpu.VMEM((2 * EXP_WIN * block, chunk), bf16),
            pltpu.VMEM((2, total, half), bf16),
            pltpu.VMEM((largest, units), jnp.float32),
            pltpu.VMEM((largest, units), bf16),
            pltpu.VMEM((2, total, half // 2), bf16),
            pltpu.VMEM((2, total, half // 2), bf16),
            pltpu.VMEM((largest, half), bf16),
            pltpu.VMEM((2 * EXP_WIN * block, chunk), bf16),
            pltpu.VMEM((2, EXP_WIN * block, chunk), bf16),
            pltpu.SemaphoreType.DMA((4,)),
            pltpu.SemaphoreType.DMA,
            pltpu.SemaphoreType.DMA((GROUP,)),
            pltpu.SemaphoreType.DMA((len(SETS),)),
            pltpu.SemaphoreType.DMA((len(SETS),)),
            pltpu.SemaphoreType.DMA((len(SETS), 2)),
            pltpu.SemaphoreType.DMA((len(SETS), 2)),
            pltpu.SemaphoreType.DMA,
            pltpu.SemaphoreType.DMA((2,)),
        ],
        compiler_params=pltpu.CompilerParams(
            collective_id=0, has_side_effects=True, vmem_limit_bytes=63 * 1024 * 1024
        ),
        cost_estimate=pl.CostEstimate(
            flops=4 * total * features * units, bytes_accessed=4 * features * units, transcendentals=0
        ),
    )(
        tokens,
        norm_gain[None, :],
        routing[None, :],
        capacity_slot[None, :],
        jnp.asarray(slot_code[:, None]),
        jnp.asarray(slot_code[None, :]),
        jnp.asarray(perm, bf16),
        jnp.asarray(perm.T, bf16),
        expert_in,
        expert_out,
    )
    return (tokens.astype(jnp.float32) + router_prob[:, None] * branch.astype(jnp.float32)).astype(jnp.bfloat16)


def per_device(tokens, routing, capacity_slot, router_prob, norm_gain, expert_in, expert_out):
    devices = lax.axis_size("expert")
    holders = devices // EXP_WIN
    features = tokens.shape[1]
    slots_total = EXP_WIN * CAP
    widened = tokens.astype(jnp.float32)
    normed = (
        widened * lax.rsqrt(jnp.mean(widened * widened, axis=-1, keepdims=True) + 1e-06) * norm_gain
    ).astype(jnp.bfloat16)
    kept_rows = capacity_slot < CAP
    target = jnp.where(kept_rows, routing * CAP + capacity_slot, -1)
    placing = (target[None, :] == jnp.arange(slots_total, dtype=jnp.int32)[:, None]).astype(
        jnp.bfloat16
    )
    buckets = (
        jnp.dot(placing, normed, preferred_element_type=jnp.float32)
        .astype(jnp.bfloat16)
        .reshape(EXP_WIN, CAP, features)
    )
    weight_in = expert_in[0]
    weight_out = expert_out[0]
    slice_width = features // holders
    sliced = (
        buckets.reshape(EXP_WIN, CAP, holders, slice_width)
        .transpose(0, 2, 1, 3)
        .reshape(devices, CAP, slice_width)
    )
    bucket_rows = lax.all_to_all(sliced, "expert", split_axis=0, concat_axis=0, tiled=True)
    lowest = lax.axis_index("expert")
    for bit_pos in range(holders.bit_length() - 1):
        partner = from_partner(bucket_rows, "expert", bit_pos)
        upper_half = lowest >> bit_pos & 1 == 1
        bucket_rows = jnp.where(
            upper_half,
            jnp.concatenate([partner, bucket_rows], 2),
            jnp.concatenate([bucket_rows, partner], 2),
        )
    slot_count = bucket_rows.shape[1]
    flat_rows = bucket_rows.reshape(devices * slot_count, features)
    hidden = jnp.maximum(
        jnp.dot(flat_rows, weight_in, preferred_element_type=jnp.float32), 0.0
    ).astype(jnp.bfloat16)
    partial_value = jnp.dot(hidden, weight_out, preferred_element_type=jnp.float32).astype(
        jnp.bfloat16
    )
    partial_value = partial_value.reshape(devices, slot_count, features)
    returned = lax.all_to_all(partial_value, "expert", split_axis=0, concat_axis=0, tiled=True)
    combined = (
        returned.reshape(EXP_WIN, holders, CAP, features)
        .astype(jnp.float32)
        .sum(axis=1)
        .reshape(slots_total, features)
    )
    picked = jnp.take(combined, jnp.clip(target, 0, slots_total - 1), axis=0)
    branch = jnp.where(kept_rows[:, None], picked, 0.0)
    return (widened + router_prob[:, None] * branch).astype(jnp.bfloat16)


def solution(mesh):
    placed = (
        P(("groups", "expert"), None),
        P(("groups", "expert")),
        P(("groups", "expert")),
        P(("groups", "expert")),
        P(),
        P("expert", None, None),
        P("expert", None, None),
    )
    two_holders = mesh.shape["expert"] == 2 * EXP_WIN
    return jax.shard_map(
        fused if two_holders else per_device,
        mesh=mesh,
        in_specs=placed,
        out_specs=P(("groups", "expert"), None),
        check_vma=False,
    )
```
